32 devices in a mesh: feat: 4 (over x, core), rows: 8 (over z, y).
Axes of the slice: x: 2, y: 2, z: 4, core: 2. Of those that a mesh axis runs over, the one named last changes fastest.
Arguments:
- kernel: float32 [8192, 8192], P('rows', 'feat'), may hold values from -0.06629126 to 5, as said below
- train_feats: float32 [4096, 8192], P('rows', 'feat'), may hold values from -6 to 6
- test_feats: float32 [2048, 8192], P('rows', 'feat'), may hold values from -6 to 6
Outputs:
- factor_state: float32 [8192, 8192], P('rows', 'feat')
- train_state: float32 [4096, 8192], P('rows', 'feat')
- test_state: float32 [2048, 8192], P('rows', 'feat')
- scores: float32 [4096, 2048], P('rows', 'feat')
The draws below stay inside these ranges and needn't reach their ends.
Inputs may be any that keep to these rules, and one draw needn't show every extreme that they name: kernel is symmetric and positive definite; its diagonal dominates each row's other entries.
All inputs are finite; a program needn't handle non-finite values.
Results may differ from the reference program's by a relative error of at most 0.0001.
Values sent between devices are 32-bit elements; how exact they have to be, the bound alone decides.
A program may use at most 128 MiB of HBM per device.

```python
import math
import jax
import jax.numpy as jnp
from jax import lax

F = 8192
PANEL = 256
NPAN = 2
TRAIN = 4096
TEST = 2048


def draw_kernel(key, part):
    entry_key, diagonal_key = jax.random.split(key)
    entries = jax.random.normal(entry_key, (F, F), jnp.float32)
    limit = 6.0 / math.sqrt(F)
    spread = jnp.clip((entries + entries.T) * (0.70710678 / math.sqrt(F)), -limit, limit)
    diagonal = jax.random.uniform(diagonal_key, (F,), jnp.float32, 3.0, 5.0)
    positions = jnp.arange(F)
    return jnp.where(positions[:, None] == positions[None, :], diagonal[:, None], spread)


def shard_levels(stream_key, dims, shards, smallest, high):
    level = 1.0
    for axis_at, blocks in shards:
        steps = jax.random.uniform(jax.random.fold_in(jax.random.fold_in(stream_key, 6), axis_at), (blocks,), jnp.float32, smallest / len(shards), high / len(shards))
        level = level * jnp.repeat(jnp.exp(steps), dims[axis_at] // blocks).reshape((-1,) + (1,) * (len(dims) - 1 - axis_at))
    return level


def scatter_about(stream_key, extent, deviation, most, pieces=(), kind=jnp.bfloat16):
    values = deviation * jax.random.normal(stream_key, extent, jnp.float32)
    if pieces:
        values = values * shard_levels(stream_key, extent, pieces, -0.22, 0.18)
    return jnp.clip(values, -most, most).astype(kind)


def setup_inputs(seed: int = 0) -> dict:
    splits = jax.random.split(jax.random.key(seed), 4)
    return {
        "kernel": draw_kernel(jax.random.fold_in(splits[3], 71), 0),
        "train_feats": scatter_about(splits[1], (TRAIN, F), 1.0, 6.0, ((0, 8), (1, 4)), jnp.float32),
        "test_feats": scatter_about(splits[2], (TEST, F), 1.0, 6.0, ((0, 8), (1, 4)), jnp.float32),
    }


def product(left, right):
    return jnp.dot(left.astype(jnp.float32), right.astype(jnp.float32), precision=lax.Precision.HIGHEST, preferred_element_type=jnp.float32)

def reference(kernel, train_feats, test_feats):
    matrix, train_work, test_work = (kernel, train_feats, test_feats)
    positions = jnp.arange(F)
    identity = jnp.eye(PANEL, dtype=jnp.float32)
    for panel in range(NPAN):
        first_col = panel * PANEL
        last_col = first_col + PANEL
        factor = jnp.linalg.cholesky(matrix[first_col:last_col, first_col:last_col])
        transposed = jax.scipy.linalg.solve_triangular(factor, identity, lower=True).T
        active = (positions >= first_col)[:, None]
        left_rows = jnp.where(active, product(matrix[:, first_col:last_col], transposed), 0.0)
        right_rows = jnp.where(active, product(matrix[first_col:last_col, :].T, transposed), 0.0)
        train_coords = product(train_work[:, first_col:last_col], transposed)
        test_coords = product(test_work[:, first_col:last_col], transposed)
        matrix = matrix - product(left_rows, right_rows.T)
        matrix = matrix.at[:, first_col:last_col].set(left_rows)
        train_work = train_work - product(train_coords, right_rows.T)
        train_work = train_work.at[:, first_col:last_col].set(train_coords)
        test_work = test_work - product(test_coords, right_rows.T)
        test_work = test_work.at[:, first_col:last_col].set(test_coords)
    coord_span = NPAN * PANEL
    upper = (positions[:, None] < coord_span) & (positions[None, :] >= coord_span)
    factor_state = jnp.where(upper, 0.0, matrix)
    scores = product(train_work[:, :coord_span], test_work[:, :coord_span].T)
    return (factor_state, train_work, test_work, scores)
```

```python
import jax
import jax.numpy as jnp
from jax import lax
from jax.experimental import pallas as pl
from jax.experimental.pallas import tpu as pltpu
from jax.sharding import PartitionSpec as P

PANEL = 256
NPAN = 2


def from_root(block, axis, holder):
    block = jnp.where(lax.axis_index(axis) == holder, block, jnp.zeros_like(block))
    return lax.psum(block, axis)


def product(left, right):
    return jnp.dot(left, right, precision=lax.Precision.HIGHEST, preferred_element_type=jnp.float32)


def update_state(state, coords, right_rows):
    return state - product(coords, right_rows.T)


def general(kernel, train_feats, test_feats):
    blk_rows, blk_cols = kernel.shape
    row_index = lax.axis_index("rows")
    feat_index = lax.axis_index("feat")
    row_ids = row_index * blk_rows + jnp.arange(blk_rows, dtype=jnp.int32)
    col_ids = feat_index * blk_cols + jnp.arange(blk_cols, dtype=jnp.int32)
    on_panel = feat_index == 0
    identity = jnp.eye(PANEL, dtype=jnp.float32)
    matrix, train_work, test_work = (kernel, train_feats, test_feats)
    train_parts = []
    test_parts = []
    pending = None
    for panel in range(NPAN):
        first_col = panel * PANEL
        last_col = first_col + PANEL
        root_row = first_col // blk_rows
        offset = first_col % blk_rows
        pending = (
            matrix[:, first_col:last_col],
            matrix[offset : offset + PANEL, :],
            train_work[:, first_col:last_col],
            test_work[:, first_col:last_col],
        )
        col_block, row_block, train_block, test_block = pending
        diagonal = from_root(col_block[offset : offset + PANEL], ("feat", "rows"), root_row)
        factor = jnp.linalg.cholesky(diagonal)
        transposed = jax.scipy.linalg.solve_triangular(factor, identity, lower=True).T
        left_rows = jnp.where((row_ids >= first_col)[:, None], product(col_block, transposed), 0.0)
        train_coords = product(train_block, transposed)
        test_coords = product(test_block, transposed)
        left_rows, train_coords, test_coords = (
            from_root(left_rows, "feat", 0),
            from_root(train_coords, "feat", 0),
            from_root(test_coords, "feat", 0),
        )
        right_rows = jnp.where(
            (col_ids >= first_col)[:, None], product(row_block.T, transposed), 0.0
        )
        right_rows = from_root(right_rows, "rows", root_row)
        train_parts.append(train_coords)
        test_parts.append(test_coords)
        pending = None
        matrix = update_state(matrix, left_rows, right_rows)
        matrix = matrix.at[:, first_col:last_col].set(
            jnp.where(on_panel, left_rows, matrix[:, first_col:last_col])
        )
        train_work = update_state(train_work, train_coords, right_rows)
        train_work = train_work.at[:, first_col:last_col].set(
            jnp.where(on_panel, train_coords, train_work[:, first_col:last_col])
        )
        test_work = update_state(test_work, test_coords, right_rows)
        test_work = test_work.at[:, first_col:last_col].set(
            jnp.where(on_panel, test_coords, test_work[:, first_col:last_col])
        )
    coord_span = NPAN * PANEL
    upper = (row_ids[:, None] < coord_span) & (col_ids[None, :] >= coord_span)
    matrix = jnp.where(upper, 0.0, matrix)
    train_all = jnp.concatenate(train_parts, axis=1)
    test_all = jnp.concatenate(test_parts, axis=1)
    groups = lax.axis_size("rows") // lax.axis_size("feat")
    every_test = lax.all_gather(test_all, "rows", axis=0, tiled=True)
    wanted = lax.dynamic_slice_in_dim(
        every_test, feat_index * (groups * test_all.shape[0]), groups * test_all.shape[0], 0
    )
    scores = product(train_all, wanted.T)
    return (matrix, train_work, test_work, scores)


SPAN = NPAN * PANEL
BASE = 128
STRIP = 8
CHUNK = 256
MESH = pl.DeviceIdType.MESH


def exact(left, right, dims):
    return lax.dot_general(
        left, right, (dims, ((), ())), precision=lax.Precision.HIGHEST, preferred_element_type=jnp.float32
    )


def base_inverse(block):
    rows = lax.broadcasted_iota(jnp.int32, (BASE, BASE), 0)
    lanes = lax.broadcasted_iota(jnp.int32, (BASE, BASE), 1)

    def strip(s, a):
        alive = rows < BASE - STRIP * s
        for j in range(STRIP):
            row = a[j : j + 1, :]
            scaled = jnp.where(lanes[:1] == j, 1.0, row) / a[j : j + 1, j : j + 1]
            below = alive & (rows > j)
            rest = jnp.where(lanes == j, 0.0, a) - a[:, j : j + 1] * scaled
            a = jnp.where(below, rest, a)
        a = jnp.concatenate([a[STRIP:], a[:STRIP]], axis=0)
        return pltpu.roll(a, BASE - STRIP, 1)

    a = lax.fori_loop(0, BASE // STRIP, strip, block)
    pivots = jnp.sum(jnp.where(rows == lanes, a, 0.0), axis=1, keepdims=True)
    scale = lax.rsqrt(pivots)
    scale = scale * (1.5 - 0.5 * pivots * scale * scale)
    return jnp.where(lanes < rows, a, jnp.where(lanes == rows, 1.0, 0.0)) * scale


def factor_step(k, work, inverse):
    lo, hi = k * BASE, (k + 1) * BASE
    corner = base_inverse(work[lo:hi, lo:hi])
    parts = []
    if k > 0:
        parts.append(exact(corner, work[lo:hi, :lo], ((1,), (0,))))
    parts.append(corner)
    done = jnp.concatenate(parts, axis=1)
    inverse[lo:hi, :hi] = done
    if hi < SPAN:
        inverse[lo:hi, hi:] = jnp.zeros((BASE, SPAN - hi), jnp.float32)
        left = exact(work[hi:, lo:hi], corner, ((1,), (1,)))
        ahead = exact(corner, work[lo:hi, hi:], ((1,), (0,)))
        work[hi:, hi:] = work[hi:, hi:] - exact(left, ahead, ((1,), (0,)))
        if k > 0:
            work[hi:, :lo] = work[hi:, :lo] - exact(left, done[:, :lo], ((1,), (0,)))
        work[hi:, lo:hi] = -exact(left, corner, ((1,), (0,)))


def gather_kernel(
    kernel, train, test, own, cross, winv, work, inverse,
    own_recv, own_core, own_x, here_recv, there_recv, up_send, down_send, side_send,
    w_recv, w_core, w_x, w_y, w_z, w_local, local_sem, diag_sem,
):
    feat, rows = lax.axis_index("feat"), lax.axis_index("rows")
    x, c = feat // 2, feat % 2
    z, y = rows // 2, rows % 2
    blk, tst, trn = kernel.shape[0], test.shape[0], train.shape[0]
    n_shared = (blk + tst) // CHUNK
    n_own = (blk + tst + trn) // CHUNK
    to_core = {"feat": 2 * x + 1 - c, "rows": rows}
    to_x = {"feat": lax.rem(feat + 2, 4), "rows": rows}
    to_y = {"feat": feat, "rows": 2 * z + 1 - y}
    to_up = {"feat": feat, "rows": jnp.minimum(rows + 2, 6 + y)}
    to_down = {"feat": feat, "rows": jnp.maximum(rows - 2, y)}
    has_up, has_down = z < 3, z > 0
    holder = feat == 0
    root = holder & (rows == 0)
    at_source = z == feat

    barrier = pltpu.get_barrier_semaphore()

    def greet(cond, target):
        @pl.when(cond)
        def _():
            pl.semaphore_signal(barrier, inc=1, device_id=target, device_id_type=MESH)

    everyone = ((True, to_core), (c == 0, to_x), (True, to_y), (has_up, to_up), (has_down, to_down))
    for cond, target in everyone:
        greet(cond, target)
    peers = 2 + jnp.where(c == 0, 1, 0) + jnp.where(has_up, 1, 0) + jnp.where(has_down, 1, 0)
    pl.semaphore_wait(barrier, peers)

    def piece(i):
        at = i * CHUNK
        if at < blk:
            return kernel.at[pl.ds(at, CHUNK), pl.ds(0, SPAN)]
        if at < blk + tst:
            return test.at[pl.ds(at - blk, CHUNK), pl.ds(0, SPAN)]
        return train.at[pl.ds(at - blk - tst, CHUNK), pl.ds(0, SPAN)]

    def own_at(i):
        return own.at[pl.ds(i * CHUNK, CHUNK), :]

    def cross_at(side, i):
        return cross.at[side, pl.ds(i * CHUNK, CHUNK), :]

    def send(src, dst, sent, received, target):
        return pltpu.make_async_remote_copy(
            src_ref=src, dst_ref=dst, send_sem=sent, recv_sem=received, device_id=target, device_id_type=MESH
        )

    def spread(src, i):
        @pl.when(has_up & (z >= feat))
        def _():
            send(src, cross_at(y, i), up_send.at[i], here_recv.at[i], to_up).start()

        @pl.when(has_down & (z <= feat))
        def _():
            send(src, cross_at(y, i), down_send.at[i], here_recv.at[i], to_down).start()

        send(src, cross_at(y, i), side_send.at[i], there_recv.at[i], to_y).start()

    diag = pltpu.make_async_copy(kernel.at[pl.ds(0, SPAN), pl.ds(0, SPAN)], work, diag_sem)

    @pl.when(root)
    def _():
        diag.start()

    @pl.when(holder)
    def _():
        for i in range(n_own):
            send(piece(i), own_at(i), own_x.at[i], own_recv.at[i], to_x).start()
            send(piece(i), own_at(i), own_core.at[i], own_recv.at[i], to_core).start()
            if i < n_shared:
                @pl.when(at_source)
                def _():
                    spread(piece(i), i)

        for i in range(n_own):
            pltpu.make_async_copy(piece(i), own_at(i), local_sem.at[i]).start()

    def w_at(k):
        return winv.at[pl.ds(k * BASE, BASE), :]

    def w_sends(k, src):
        rows_k = w_at(k)
        return (
            (holder & (y == 0) & has_up, send(src, rows_k, w_z.at[k], w_recv.at[k], to_up)),
            (holder & (y == 0), send(src, rows_k, w_y.at[k], w_recv.at[k], to_y)),
            (holder, send(src, rows_k, w_x.at[k], w_recv.at[k], to_x)),
            (c == 0, send(src, rows_k, w_core.at[k], w_recv.at[k], to_core)),
        )

    @pl.when(root)
    def _():
        diag.wait()
        for k in range(SPAN // BASE):
            factor_step(k, work, inverse)
            src = inverse.at[pl.ds(k * BASE, BASE), :]
            for cond, copy in w_sends(k, src):
                @pl.when(cond)
                def _():
                    copy.start()
            pltpu.make_async_copy(src, w_at(k), w_local.at[k]).start()

    for i in range(n_own):
        @pl.when(feat != 0)
        def _():
            send(own_at(i), own_at(i), own_x.at[i], own_recv.at[i], to_core).wait_recv()

        @pl.when(feat == 2)
        def _():
            send(own_at(i), own_at(i), own_core.at[i], own_recv.at[i], to_core).start()

        if i < n_shared:
            @pl.when(at_source & (feat != 0))
            def _():
                spread(own_at(i), i)

            @pl.when(jnp.logical_not(at_source))
            def _():
                send(cross_at(y, i), cross_at(y, i), side_send.at[i], here_recv.at[i], to_y).wait_recv()
                spread(cross_at(y, i), i)

    @pl.when(holder)
    def _():
        for i in range(n_own):
            pltpu.make_async_copy(piece(i), own_at(i), local_sem.at[i]).wait()

    @pl.when(at_source)
    def _():
        for i in range(n_shared):
            pltpu.make_async_copy(own_at(i), cross_at(y, i), here_recv.at[i]).start()

    for k in range(SPAN // BASE):
        @pl.when(jnp.logical_not(root))
        def _():
            send(w_at(k), w_at(k), w_core.at[k], w_recv.at[k], to_core).wait_recv()
            for cond, copy in w_sends(k, w_at(k)):
                @pl.when(cond)
                def _():
                    copy.start()

    for k in range(SPAN // BASE):
        for cond, copy in w_sends(k, w_at(k)):
            @pl.when(cond)
            def _():
                copy.wait_send()

        @pl.when(root)
        def _():
            pltpu.make_async_copy(w_at(k), w_at(k), w_local.at[k]).wait()

    for i in range(n_own):
        @pl.when(holder)
        def _():
            send(own_at(i), own_at(i), own_x.at[i], own_recv.at[i], to_x).wait_send()

        @pl.when(c == 0)
        def _():
            send(own_at(i), own_at(i), own_core.at[i], own_recv.at[i], to_core).wait_send()

    for i in range(n_shared):
        @pl.when(at_source)
        def _():
            pltpu.make_async_copy(own_at(i), cross_at(y, i), here_recv.at[i]).wait()

        @pl.when(has_up & (z >= feat))
        def _():
            send(own_at(i), cross_at(y, i), up_send.at[i], here_recv.at[i], to_up).wait_send()

        @pl.when(has_down & (z <= feat))
        def _():
            send(own_at(i), cross_at(y, i), down_send.at[i], here_recv.at[i], to_down).wait_send()

        side = send(own_at(i), cross_at(1 - y, i), side_send.at[i], there_recv.at[i], to_y)
        side.wait_send()
        side.wait_recv()


def gather(kernel, train, test):
    blk, tst, trn = kernel.shape[0], test.shape[0], train.shape[0]
    n_shared = (blk + tst) // CHUNK
    n_own = (blk + tst + trn) // CHUNK
    n_w = SPAN // BASE
    dma = pltpu.SemaphoreType.DMA
    anywhere = pl.BlockSpec(memory_space=pl.ANY)
    return pl.pallas_call(
        gather_kernel,
        out_shape=(
            jax.ShapeDtypeStruct((blk + tst + trn, SPAN), jnp.float32),
            jax.ShapeDtypeStruct((2, blk + tst, SPAN), jnp.float32),
            jax.ShapeDtypeStruct((SPAN, SPAN), jnp.float32),
        ),
        in_specs=[anywhere] * 3,
        out_specs=(anywhere,) * 3,
        scratch_shapes=[
            pltpu.VMEM((SPAN, SPAN), jnp.float32),
            pltpu.VMEM((SPAN, SPAN), jnp.float32),
            dma((n_own,)), dma((n_own,)), dma((n_own,)),
            dma((n_shared,)), dma((n_shared,)), dma((n_shared,)), dma((n_shared,)), dma((n_shared,)),
            dma((n_w,)), dma((n_w,)), dma((n_w,)), dma((n_w,)), dma((n_w,)), dma((n_w,)),
            dma((n_own,)), dma,
        ],
        compiler_params=pltpu.CompilerParams(
            collective_id=0, has_side_effects=True, vmem_limit_bytes=24 * 1024 * 1024
        ),
    )(kernel, train, test)


def fast(left, right):
    return lax.dot_general(
        left, right, (((1,), (1,)), ((), ())), precision=lax.Precision.HIGH, preferred_element_type=jnp.float32
    )


def per_device(kernel, train_feats, test_feats):
    blk, blk_cols = kernel.shape
    tst, trn = test_feats.shape[0], train_feats.shape[0]
    row_ids = lax.axis_index("rows") * blk + lax.broadcasted_iota(jnp.int32, (blk, 1), 0)
    col_ids = lax.axis_index("feat") * blk_cols + lax.broadcasted_iota(jnp.int32, (1, blk_cols), 1)
    own, cross, winv = gather(kernel, train_feats, test_feats)
    coords = fast(own, winv)
    panel_of = (jnp.arange(SPAN, dtype=jnp.int32) // PANEL) * PANEL
    left = jnp.where(row_ids >= panel_of[None, :], coords[:blk], 0.0)
    test_coords, train_coords = coords[blk : blk + tst], coords[blk + tst :]
    other = fast(cross.reshape(2 * (blk + tst), SPAN), winv).reshape(2, blk + tst, SPAN)
    right = other[:, :blk].reshape(2 * blk, SPAN)
    scored = other[:, blk:].reshape(2 * tst, SPAN)

    def updated(state, part):
        rest = state - fast(part, right)
        padded = jnp.pad(part, ((0, 0), (0, blk_cols - SPAN)))
        return jnp.where(col_ids < SPAN, padded, rest)

    matrix = jnp.where((row_ids < SPAN) & (col_ids >= SPAN), 0.0, updated(kernel, left))
    return (
        matrix,
        updated(train_feats, train_coords),
        updated(test_feats, test_coords),
        fast(train_coords, scored),
    )


def solution(mesh):
    wide = mesh.shape["feat"] == 4 and mesh.shape["rows"] == 8
    return jax.shard_map(
        per_device if wide else general,
        mesh=mesh,
        in_specs=(P("rows", "feat"), P("rows", "feat"), P("rows", "feat")),
        out_specs=(P("rows", "feat"), P("rows", "feat"), P("rows", "feat"), P("rows", "feat")),
        check_vma=False,
    )
```

```python
import jax
import jax.numpy as jnp
from jax import lax
from jax.experimental import pallas as pl
from jax.experimental.pallas import tpu as pltpu
from jax.sharding import PartitionSpec as P

PANEL = 256
NPAN = 2


def from_root(block, axis, holder):
    block = jnp.where(lax.axis_index(axis) == holder, block, jnp.zeros_like(block))
    return lax.psum(block, axis)


def product(left, right):
    return jnp.dot(left, right, precision=lax.Precision.HIGHEST, preferred_element_type=jnp.float32)


def update_state(state, coords, right_rows):
    return state - product(coords, right_rows.T)


def general(kernel, train_feats, test_feats):
    blk_rows, blk_cols = kernel.shape
    row_index = lax.axis_index("rows")
    feat_index = lax.axis_index("feat")
    row_ids = row_index * blk_rows + jnp.arange(blk_rows, dtype=jnp.int32)
    col_ids = feat_index * blk_cols + jnp.arange(blk_cols, dtype=jnp.int32)
    on_panel = feat_index == 0
    identity = jnp.eye(PANEL, dtype=jnp.float32)
    matrix, train_work, test_work = (kernel, train_feats, test_feats)
    train_parts = []
    test_parts = []
    pending = None
    for panel in range(NPAN):
        first_col = panel * PANEL
        last_col = first_col + PANEL
        root_row = first_col // blk_rows
        offset = first_col % blk_rows
        pending = (
            matrix[:, first_col:last_col],
            matrix[offset : offset + PANEL, :],
            train_work[:, first_col:last_col],
            test_work[:, first_col:last_col],
        )
        col_block, row_block, train_block, test_block = pending
        diagonal = from_root(col_block[offset : offset + PANEL], ("feat", "rows"), root_row)
        factor = jnp.linalg.cholesky(diagonal)
        transposed = jax.scipy.linalg.solve_triangular(factor, identity, lower=True).T
        left_rows = jnp.where((row_ids >= first_col)[:, None], product(col_block, transposed), 0.0)
        train_coords = product(train_block, transposed)
        test_coords = product(test_block, transposed)
        left_rows, train_coords, test_coords = (
            from_root(left_rows, "feat", 0),
            from_root(train_coords, "feat", 0),
            from_root(test_coords, "feat", 0),
        )
        right_rows = jnp.where(
            (col_ids >= first_col)[:, None], product(row_block.T, transposed), 0.0
        )
        right_rows = from_root(right_rows, "rows", root_row)
        train_parts.append(train_coords)
        test_parts.append(test_coords)
        pending = None
        matrix = update_state(matrix, left_rows, right_rows)
        matrix = matrix.at[:, first_col:last_col].set(
            jnp.where(on_panel, left_rows, matrix[:, first_col:last_col])
        )
        train_work = update_state(train_work, train_coords, right_rows)
        train_work = train_work.at[:, first_col:last_col].set(
            jnp.where(on_panel, train_coords, train_work[:, first_col:last_col])
        )
        test_work = update_state(test_work, test_coords, right_rows)
        test_work = test_work.at[:, first_col:last_col].set(
            jnp.where(on_panel, test_coords, test_work[:, first_col:last_col])
        )
    coord_span = NPAN * PANEL
    upper = (row_ids[:, None] < coord_span) & (col_ids[None, :] >= coord_span)
    matrix = jnp.where(upper, 0.0, matrix)
    train_all = jnp.concatenate(train_parts, axis=1)
    test_all = jnp.concatenate(test_parts, axis=1)
    groups = lax.axis_size("rows") // lax.axis_size("feat")
    every_test = lax.all_gather(test_all, "rows", axis=0, tiled=True)
    wanted = lax.dynamic_slice_in_dim(
        every_test, feat_index * (groups * test_all.shape[0]), groups * test_all.shape[0], 0
    )
    scores = product(train_all, wanted.T)
    return (matrix, train_work, test_work, scores)


SPAN = NPAN * PANEL
BASE = 128
STRIP = 8
CHUNK = 256
PIECE = 64
MESH = pl.DeviceIdType.MESH


def exact(left, right, dims):
    return lax.dot_general(
        left, right, (dims, ((), ())), precision=lax.Precision.HIGHEST, preferred_element_type=jnp.float32
    )


def base_inverse(block):
    rows = lax.broadcasted_iota(jnp.int32, (BASE, BASE), 0)
    lanes = lax.broadcasted_iota(jnp.int32, (BASE, BASE), 1)

    def strip(s, a):
        alive = rows < BASE - STRIP * s
        for j in range(STRIP):
            row = a[j : j + 1, :]
            scaled = jnp.where(lanes[:1] == j, 1.0, row) / a[j : j + 1, j : j + 1]
            below = alive & (rows > j)
            rest = jnp.where(lanes == j, 0.0, a) - a[:, j : j + 1] * scaled
            a = jnp.where(below, rest, a)
        a = jnp.concatenate([a[STRIP:], a[:STRIP]], axis=0)
        return pltpu.roll(a, BASE - STRIP, 1)

    a = lax.fori_loop(0, BASE // STRIP, strip, block)
    pivots = jnp.sum(jnp.where(rows == lanes, a, 0.0), axis=1, keepdims=True)
    scale = lax.rsqrt(pivots)
    scale = scale * (1.5 - 0.5 * pivots * scale * scale)
    return jnp.where(lanes < rows, a, jnp.where(lanes == rows, 1.0, 0.0)) * scale


def factor_step(k, work, inverse):
    lo, hi = k * BASE, (k + 1) * BASE
    corner = base_inverse(work[lo:hi, lo:hi])
    parts = []
    if k > 0:
        parts.append(exact(corner, work[lo:hi, :lo], ((1,), (0,))))
    parts.append(corner)
    done = jnp.concatenate(parts, axis=1)
    inverse[lo:hi, :hi] = done
    if hi < SPAN:
        inverse[lo:hi, hi:] = jnp.zeros((BASE, SPAN - hi), jnp.float32)
        left = exact(work[hi:, lo:hi], corner, ((1,), (1,)))
        ahead = exact(corner, work[lo:hi, hi:], ((1,), (0,)))
        work[hi:, hi:] = work[hi:, hi:] - exact(left, ahead, ((1,), (0,)))
        if k > 0:
            work[hi:, :lo] = work[hi:, :lo] - exact(left, done[:, :lo], ((1,), (0,)))
        work[hi:, lo:hi] = -exact(left, corner, ((1,), (0,)))


def gather_kernel(
    kernel, train, test, own, cross, winv, work, inverse,
    own_recv, own_core, own_x, here_recv, there_recv, up_send, down_send, side_send,
    w_recv, w_core, w_x, w_y, w_z, w_local, local_sem, diag_sem,
):
    feat, rows = lax.axis_index("feat"), lax.axis_index("rows")
    x, c = feat // 2, feat % 2
    z, y = rows // 2, rows % 2
    blk, tst, trn = kernel.shape[0], test.shape[0], train.shape[0]
    n_shared = (blk + tst) // CHUNK
    n_own = (blk + tst + trn) // CHUNK
    to_core = {"feat": 2 * x + 1 - c, "rows": rows}
    to_x = {"feat": lax.rem(feat + 2, 4), "rows": rows}
    to_y = {"feat": feat, "rows": 2 * z + 1 - y}
    to_up = {"feat": feat, "rows": jnp.minimum(rows + 2, 6 + y)}
    to_down = {"feat": feat, "rows": jnp.maximum(rows - 2, y)}
    has_up, has_down = z < 3, z > 0
    holder = feat == 0
    root = holder & (rows == 0)
    at_source = z == feat

    barrier = pltpu.get_barrier_semaphore()

    def greet(cond, target):
        @pl.when(cond)
        def _():
            pl.semaphore_signal(barrier, inc=1, device_id=target, device_id_type=MESH)

    everyone = ((True, to_core), (c == 0, to_x), (True, to_y), (has_up, to_up), (has_down, to_down))
    for cond, target in everyone:
        greet(cond, target)
    peers = 2 + jnp.where(c == 0, 1, 0) + jnp.where(has_up, 1, 0) + jnp.where(has_down, 1, 0)
    pl.semaphore_wait(barrier, peers)

    def piece(i):
        at = i * CHUNK
        if at < blk:
            return kernel.at[pl.ds(at, CHUNK), pl.ds(0, SPAN)]
        if at < blk + tst:
            return test.at[pl.ds(at - blk, CHUNK), pl.ds(0, SPAN)]
        return train.at[pl.ds(at - blk - tst, CHUNK), pl.ds(0, SPAN)]

    def own_at(i):
        return own.at[pl.ds(i * CHUNK, CHUNK), :]

    def cross_at(side, i):
        return cross.at[side, pl.ds(i * CHUNK, CHUNK), :]

    def send(src, dst, sent, received, target):
        return pltpu.make_async_remote_copy(
            src_ref=src, dst_ref=dst, send_sem=sent, recv_sem=received, device_id=target, device_id_type=MESH
        )

    def spread(src, i):
        @pl.when(has_up & (z >= feat))
        def _():
            send(src, cross_at(y, i), up_send.at[i], here_recv.at[i], to_up).start()

        @pl.when(has_down & (z <= feat))
        def _():
            send(src, cross_at(y, i), down_send.at[i], here_recv.at[i], to_down).start()

        send(src, cross_at(y, i), side_send.at[i], there_recv.at[i], to_y).start()

    diag = pltpu.make_async_copy(kernel.at[pl.ds(0, SPAN), pl.ds(0, SPAN)], work, diag_sem)

    @pl.when(root)
    def _():
        diag.start()

    @pl.when(holder)
    def _():
        for i in range(n_own):
            send(piece(i), own_at(i), own_x.at[i], own_recv.at[i], to_x).start()
            send(piece(i), own_at(i), own_core.at[i], own_recv.at[i], to_core).start()
            if i < n_shared:
                @pl.when(at_source)
                def _():
                    spread(piece(i), i)

        for i in range(n_own):
            pltpu.make_async_copy(piece(i), own_at(i), local_sem.at[i]).start()

    def w_at(k):
        return winv.at[pl.ds(k * PIECE, PIECE), :]

    def w_sends(k, src):
        rows_k = w_at(k)
        return (
            (holder & (y == 0) & has_up, send(src, rows_k, w_z.at[k], w_recv.at[k], to_up)),
            (holder & (y == 0), send(src, rows_k, w_y.at[k], w_recv.at[k], to_y)),
            (holder, send(src, rows_k, w_x.at[k], w_recv.at[k], to_x)),
            (c == 0, send(src, rows_k, w_core.at[k], w_recv.at[k], to_core)),
        )

    @pl.when(root)
    def _():
        diag.wait()
        for k in range(SPAN // BASE):
            factor_step(k, work, inverse)
            for part in range(k * BASE // PIECE, (k + 1) * BASE // PIECE):
                src = inverse.at[pl.ds(part * PIECE, PIECE), :]
                for cond, copy in w_sends(part, src):
                    @pl.when(cond)
                    def _():
                        copy.start()
                pltpu.make_async_copy(src, w_at(part), w_local.at[part]).start()

    for i in range(n_own):
        @pl.when(feat != 0)
        def _():
            send(own_at(i), own_at(i), own_x.at[i], own_recv.at[i], to_core).wait_recv()

        @pl.when(feat == 2)
        def _():
            send(own_at(i), own_at(i), own_core.at[i], own_recv.at[i], to_core).start()

        if i < n_shared:
            @pl.when(at_source & (feat != 0))
            def _():
                spread(own_at(i), i)

            @pl.when(jnp.logical_not(at_source))
            def _():
                send(cross_at(y, i), cross_at(y, i), side_send.at[i], here_recv.at[i], to_y).wait_recv()
                spread(cross_at(y, i), i)

    @pl.when(holder)
    def _():
        for i in range(n_own):
            pltpu.make_async_copy(piece(i), own_at(i), local_sem.at[i]).wait()

    @pl.when(at_source)
    def _():
        for i in range(n_shared):
            pltpu.make_async_copy(own_at(i), cross_at(y, i), here_recv.at[i]).start()

    for k in range(SPAN // PIECE):
        @pl.when(jnp.logical_not(root))
        def _():
            send(w_at(k), w_at(k), w_core.at[k], w_recv.at[k], to_core).wait_recv()
            for cond, copy in w_sends(k, w_at(k)):
                @pl.when(cond)
                def _():
                    copy.start()

    for k in range(SPAN // PIECE):
        for cond, copy in w_sends(k, w_at(k)):
            @pl.when(cond)
            def _():
                copy.wait_send()

        @pl.when(root)
        def _():
            pltpu.make_async_copy(w_at(k), w_at(k), w_local.at[k]).wait()

    for i in range(n_own):
        @pl.when(holder)
        def _():
            send(own_at(i), own_at(i), own_x.at[i], own_recv.at[i], to_x).wait_send()

        @pl.when(c == 0)
        def _():
            send(own_at(i), own_at(i), own_core.at[i], own_recv.at[i], to_core).wait_send()

    for i in range(n_shared):
        @pl.when(at_source)
        def _():
            pltpu.make_async_copy(own_at(i), cross_at(y, i), here_recv.at[i]).wait()

        @pl.when(has_up & (z >= feat))
        def _():
            send(own_at(i), cross_at(y, i), up_send.at[i], here_recv.at[i], to_up).wait_send()

        @pl.when(has_down & (z <= feat))
        def _():
            send(own_at(i), cross_at(y, i), down_send.at[i], here_recv.at[i], to_down).wait_send()

        side = send(own_at(i), cross_at(1 - y, i), side_send.at[i], there_recv.at[i], to_y)
        side.wait_send()
        side.wait_recv()


def gather(kernel, train, test):
    blk, tst, trn = kernel.shape[0], test.shape[0], train.shape[0]
    n_shared = (blk + tst) // CHUNK
    n_own = (blk + tst + trn) // CHUNK
    n_w = SPAN // PIECE
    dma = pltpu.SemaphoreType.DMA
    anywhere = pl.BlockSpec(memory_space=pl.ANY)
    return pl.pallas_call(
        gather_kernel,
        out_shape=(
            jax.ShapeDtypeStruct((blk + tst + trn, SPAN), jnp.float32),
            jax.ShapeDtypeStruct((2, blk + tst, SPAN), jnp.float32),
            jax.ShapeDtypeStruct((SPAN, SPAN), jnp.float32),
        ),
        in_specs=[anywhere] * 3,
        out_specs=(anywhere,) * 3,
        scratch_shapes=[
            pltpu.VMEM((SPAN, SPAN), jnp.float32),
            pltpu.VMEM((SPAN, SPAN), jnp.float32),
            dma((n_own,)), dma((n_own,)), dma((n_own,)),
            dma((n_shared,)), dma((n_shared,)), dma((n_shared,)), dma((n_shared,)), dma((n_shared,)),
            dma((n_w,)), dma((n_w,)), dma((n_w,)), dma((n_w,)), dma((n_w,)), dma((n_w,)),
            dma((n_own,)), dma,
        ],
        compiler_params=pltpu.CompilerParams(
            collective_id=0, has_side_effects=True, vmem_limit_bytes=44 * 1024 * 1024
        ),
    )(kernel, train, test)


def fast(left, right):
    return lax.dot_general(
        left, right, (((1,), (1,)), ((), ())), precision=lax.Precision.HIGH, preferred_element_type=jnp.float32
    )


def per_device(kernel, train_feats, test_feats):
    blk, blk_cols = kernel.shape
    tst, trn = test_feats.shape[0], train_feats.shape[0]
    row_ids = lax.axis_index("rows") * blk + lax.broadcasted_iota(jnp.int32, (blk, 1), 0)
    col_ids = lax.axis_index("feat") * blk_cols + lax.broadcasted_iota(jnp.int32, (1, blk_cols), 1)
    own, cross, winv = gather(kernel, train_feats, test_feats)
    coords = fast(own, winv)
    panel_of = (jnp.arange(SPAN, dtype=jnp.int32) // PANEL) * PANEL
    left = jnp.where(row_ids >= panel_of[None, :], coords[:blk], 0.0)
    test_coords, train_coords = coords[blk : blk + tst], coords[blk + tst :]
    other = fast(cross.reshape(2 * (blk + tst), SPAN), winv).reshape(2, blk + tst, SPAN)
    right = other[:, :blk].reshape(2 * blk, SPAN)
    scored = other[:, blk:].reshape(2 * tst, SPAN)

    def updated(state, part):
        rest = state - fast(part, right)
        padded = jnp.pad(part, ((0, 0), (0, blk_cols - SPAN)))
        return jnp.where(col_ids < SPAN, padded, rest)

    matrix = jnp.where((row_ids < SPAN) & (col_ids >= SPAN), 0.0, updated(kernel, left))
    return (
        matrix,
        updated(train_feats, train_coords),
        updated(test_feats, test_coords),
        fast(train_coords, scored),
    )


def solution(mesh):
    wide = mesh.shape["feat"] == 4 and mesh.shape["rows"] == 8
    return jax.shard_map(
        per_device if wide else general,
        mesh=mesh,
        in_specs=(P("rows", "feat"), P("rows", "feat"), P("rows", "feat")),
        out_specs=(P("rows", "feat"), P("rows", "feat"), P("rows", "feat"), P("rows", "feat")),
        check_vma=False,
    )
```

```python
import jax
import jax.numpy as jnp
from jax import lax
from jax.experimental import pallas as pl
from jax.experimental.pallas import tpu as pltpu
from jax.sharding import PartitionSpec as P

PANEL = 256
NPAN = 2


def from_root(block, axis, holder):
    block = jnp.where(lax.axis_index(axis) == holder, block, jnp.zeros_like(block))
    return lax.psum(block, axis)


def product(left, right):
    return jnp.dot(left, right, precision=lax.Precision.HIGHEST, preferred_element_type=jnp.float32)


def update_state(state, coords, right_rows):
    return state - product(coords, right_rows.T)


def general(kernel, train_feats, test_feats):
    blk_rows, blk_cols = kernel.shape
    row_index = lax.axis_index("rows")
    feat_index = lax.axis_index("feat")
    row_ids = row_index * blk_rows + jnp.arange(blk_rows, dtype=jnp.int32)
    col_ids = feat_index * blk_cols + jnp.arange(blk_cols, dtype=jnp.int32)
    on_panel = feat_index == 0
    identity = jnp.eye(PANEL, dtype=jnp.float32)
    matrix, train_work, test_work = (kernel, train_feats, test_feats)
    train_parts = []
    test_parts = []
    pending = None
    for panel in range(NPAN):
        first_col = panel * PANEL
        last_col = first_col + PANEL
        root_row = first_col // blk_rows
        offset = first_col % blk_rows
        pending = (
            matrix[:, first_col:last_col],
            matrix[offset : offset + PANEL, :],
            train_work[:, first_col:last_col],
            test_work[:, first_col:last_col],
        )
        col_block, row_block, train_block, test_block = pending
        diagonal = from_root(col_block[offset : offset + PANEL], ("feat", "rows"), root_row)
        factor = jnp.linalg.cholesky(diagonal)
        transposed = jax.scipy.linalg.solve_triangular(factor, identity, lower=True).T
        left_rows = jnp.where((row_ids >= first_col)[:, None], product(col_block, transposed), 0.0)
        train_coords = product(train_block, transposed)
        test_coords = product(test_block, transposed)
        left_rows, train_coords, test_coords = (
            from_root(left_rows, "feat", 0),
            from_root(train_coords, "feat", 0),
            from_root(test_coords, "feat", 0),
        )
        right_rows = jnp.where(
            (col_ids >= first_col)[:, None], product(row_block.T, transposed), 0.0
        )
        right_rows = from_root(right_rows, "rows", root_row)
        train_parts.append(train_coords)
        test_parts.append(test_coords)
        pending = None
        matrix = update_state(matrix, left_rows, right_rows)
        matrix = matrix.at[:, first_col:last_col].set(
            jnp.where(on_panel, left_rows, matrix[:, first_col:last_col])
        )
        train_work = update_state(train_work, train_coords, right_rows)
        train_work = train_work.at[:, first_col:last_col].set(
            jnp.where(on_panel, train_coords, train_work[:, first_col:last_col])
        )
        test_work = update_state(test_work, test_coords, right_rows)
        test_work = test_work.at[:, first_col:last_col].set(
            jnp.where(on_panel, test_coords, test_work[:, first_col:last_col])
        )
    coord_span = NPAN * PANEL
    upper = (row_ids[:, None] < coord_span) & (col_ids[None, :] >= coord_span)
    matrix = jnp.where(upper, 0.0, matrix)
    train_all = jnp.concatenate(train_parts, axis=1)
    test_all = jnp.concatenate(test_parts, axis=1)
    groups = lax.axis_size("rows") // lax.axis_size("feat")
    every_test = lax.all_gather(test_all, "rows", axis=0, tiled=True)
    wanted = lax.dynamic_slice_in_dim(
        every_test, feat_index * (groups * test_all.shape[0]), groups * test_all.shape[0], 0
    )
    scores = product(train_all, wanted.T)
    return (matrix, train_work, test_work, scores)


SPAN = NPAN * PANEL
BASE = 128
STRIP = 8
CHUNK = 256
PIECE = 64
MESH = pl.DeviceIdType.MESH


def exact(left, right, dims):
    return lax.dot_general(
        left, right, (dims, ((), ())), precision=lax.Precision.HIGHEST, preferred_element_type=jnp.float32
    )


def base_inverse(block):
    rows = lax.broadcasted_iota(jnp.int32, (BASE, BASE), 0)
    lanes = lax.broadcasted_iota(jnp.int32, (BASE, BASE), 1)

    def strip(s, a):
        alive = rows < BASE - STRIP * s
        for j in range(STRIP):
            row = a[j : j + 1, :]
            scaled = jnp.where(lanes[:1] == j, 1.0, row) / a[j : j + 1, j : j + 1]
            below = alive & (rows > j)
            rest = jnp.where(lanes == j, 0.0, a) - a[:, j : j + 1] * scaled
            a = jnp.where(below, rest, a)
        a = jnp.concatenate([a[STRIP:], a[:STRIP]], axis=0)
        return pltpu.roll(a, BASE - STRIP, 1)

    a = lax.fori_loop(0, BASE // STRIP, strip, block)
    pivots = jnp.sum(jnp.where(rows == lanes, a, 0.0), axis=1, keepdims=True)
    scale = lax.rsqrt(pivots)
    scale = scale * (1.5 - 0.5 * pivots * scale * scale)
    return jnp.where(lanes < rows, a, jnp.where(lanes == rows, 1.0, 0.0)) * scale


def factor_step(k, work, inverse):
    lo, hi = k * BASE, (k + 1) * BASE
    corner = base_inverse(work[lo:hi, lo:hi])
    parts = []
    if k > 0:
        parts.append(exact(corner, work[lo:hi, :lo], ((1,), (0,))))
    parts.append(corner)
    done = jnp.concatenate(parts, axis=1)
    inverse[lo:hi, :hi] = done
    if hi < SPAN:
        inverse[lo:hi, hi:] = jnp.zeros((BASE, SPAN - hi), jnp.float32)
        left = exact(work[hi:, lo:hi], corner, ((1,), (1,)))
        ahead = exact(corner, work[lo:hi, hi:], ((1,), (0,)))
        work[hi:, hi:] = work[hi:, hi:] - exact(left, ahead, ((1,), (0,)))
        if k > 0:
            work[hi:, :lo] = work[hi:, :lo] - exact(left, done[:, :lo], ((1,), (0,)))
        work[hi:, lo:hi] = -exact(left, corner, ((1,), (0,)))


def gather_kernel(
    kernel, train, test, own, cross, winv, work, inverse,
    own_recv, own_core, own_x, here_recv, there_recv, up_send, down_send, side_send,
    w_recv, w_core, w_x, w_y, w_z, w_local, local_sem, diag_sem,
):
    feat, rows = lax.axis_index("feat"), lax.axis_index("rows")
    x, c = feat // 2, feat % 2
    z, y = rows // 2, rows % 2
    blk, tst, trn = kernel.shape[0], test.shape[0], train.shape[0]
    n_shared = (blk + tst) // CHUNK
    n_own = (blk + tst + trn) // CHUNK
    to_core = {"feat": 2 * x + 1 - c, "rows": rows}
    to_x = {"feat": lax.rem(feat + 2, 4), "rows": rows}
    to_y = {"feat": feat, "rows": 2 * z + 1 - y}
    to_up = {"feat": feat, "rows": jnp.minimum(rows + 2, 6 + y)}
    to_down = {"feat": feat, "rows": jnp.maximum(rows - 2, y)}
    has_up, has_down = z < 3, z > 0
    holder = feat == 0
    root = holder & (rows == 0)
    at_source = z == feat

    barrier = pltpu.get_barrier_semaphore()

    def greet(cond, target):
        @pl.when(cond)
        def _():
            pl.semaphore_signal(barrier, inc=1, device_id=target, device_id_type=MESH)

    everyone = ((True, to_core), (c == 0, to_x), (True, to_y), (has_up, to_up), (has_down, to_down))
    for cond, target in everyone:
        greet(cond, target)
    peers = 2 + jnp.where(c == 0, 1, 0) + jnp.where(has_up, 1, 0) + jnp.where(has_down, 1, 0)
    pl.semaphore_wait(barrier, peers)

    def piece(i):
        at = i * CHUNK
        if at < blk:
            return kernel.at[pl.ds(at, CHUNK), pl.ds(0, SPAN)]
        if at < blk + tst:
            return test.at[pl.ds(at - blk, CHUNK), pl.ds(0, SPAN)]
        return train.at[pl.ds(at - blk - tst, CHUNK), pl.ds(0, SPAN)]

    def own_at(i):
        return own.at[pl.ds(i * CHUNK, CHUNK), :]

    def cross_at(side, i):
        return cross.at[side, pl.ds(i * CHUNK, CHUNK), :]

    def send(src, dst, sent, received, target):
        return pltpu.make_async_remote_copy(
            src_ref=src, dst_ref=dst, send_sem=sent, recv_sem=received, device_id=target, device_id_type=MESH
        )

    def spread(src, i):
        @pl.when(has_up & (z >= feat))
        def _():
            send(src, cross_at(y, i), up_send.at[i], here_recv.at[i], to_up).start()

        @pl.when(has_down & (z <= feat))
        def _():
            send(src, cross_at(y, i), down_send.at[i], here_recv.at[i], to_down).start()

        send(src, cross_at(y, i), side_send.at[i], there_recv.at[i], to_y).start()

    diag = pltpu.make_async_copy(kernel.at[pl.ds(0, SPAN), pl.ds(0, SPAN)], work, diag_sem)

    @pl.when(root)
    def _():
        diag.start()

    @pl.when(holder)
    def _():
        for i in range(n_own):
            send(piece(i), own_at(i), own_x.at[i], own_recv.at[i], to_x).start()
            send(piece(i), own_at(i), own_core.at[i], own_recv.at[i], to_core).start()
            if i < n_shared:
                @pl.when(at_source)
                def _():
                    spread(piece(i), i)

        for i in range(n_own):
            pltpu.make_async_copy(piece(i), own_at(i), local_sem.at[i]).start()

    def w_at(k):
        return winv.at[pl.ds(k * PIECE, PIECE), :]

    def w_sends(k, src):
        rows_k = w_at(k)
        return (
            (holder & (y == 0) & has_up, send(src, rows_k, w_z.at[k], w_recv.at[k], to_up)),
            (holder & (y == 0), send(src, rows_k, w_y.at[k], w_recv.at[k], to_y)),
            (holder, send(src, rows_k, w_x.at[k], w_recv.at[k], to_x)),
            (c == 0, send(src, rows_k, w_core.at[k], w_recv.at[k], to_core)),
        )

    @pl.when(root)
    def _():
        diag.wait()
        for k in range(SPAN // BASE):
            factor_step(k, work, inverse)
            for part in range(k * BASE // PIECE, (k + 1) * BASE // PIECE):
                src = inverse.at[pl.ds(part * PIECE, PIECE), :]
                for cond, copy in w_sends(part, src):
                    @pl.when(cond)
                    def _():
                        copy.start()
                pltpu.make_async_copy(src, w_at(part), w_local.at[part]).start()

    def relay(k):
        @pl.when(jnp.logical_not(root))
        def _():
            send(w_at(k), w_at(k), w_core.at[k], w_recv.at[k], to_core).wait_recv()
            for cond, copy in w_sends(k, w_at(k)):
                @pl.when(cond)
                def _():
                    copy.start()

    for i in range(n_own):
        if 2 <= i <= 4:
            for k in range((i - 2) * BASE // PIECE, (i - 1) * BASE // PIECE):
                relay(k)

        @pl.when(feat != 0)
        def _():
            send(own_at(i), own_at(i), own_x.at[i], own_recv.at[i], to_core).wait_recv()

        @pl.when(feat == 2)
        def _():
            send(own_at(i), own_at(i), own_core.at[i], own_recv.at[i], to_core).start()

        if i < n_shared:
            @pl.when(at_source & (feat != 0))
            def _():
                spread(own_at(i), i)

            @pl.when(jnp.logical_not(at_source))
            def _():
                send(cross_at(y, i), cross_at(y, i), side_send.at[i], here_recv.at[i], to_y).wait_recv()
                spread(cross_at(y, i), i)

    @pl.when(holder)
    def _():
        for i in range(n_own):
            pltpu.make_async_copy(piece(i), own_at(i), local_sem.at[i]).wait()

    @pl.when(at_source)
    def _():
        for i in range(n_shared):
            pltpu.make_async_copy(own_at(i), cross_at(y, i), here_recv.at[i]).start()

    for k in range(3 * BASE // PIECE, SPAN // PIECE):
        relay(k)

    for k in range(SPAN // PIECE):
        for cond, copy in w_sends(k, w_at(k)):
            @pl.when(cond)
            def _():
                copy.wait_send()

        @pl.when(root)
        def _():
            pltpu.make_async_copy(w_at(k), w_at(k), w_local.at[k]).wait()

    for i in range(n_own):
        @pl.when(holder)
        def _():
            send(own_at(i), own_at(i), own_x.at[i], own_recv.at[i], to_x).wait_send()

        @pl.when(c == 0)
        def _():
            send(own_at(i), own_at(i), own_core.at[i], own_recv.at[i], to_core).wait_send()

    for i in range(n_shared):
        @pl.when(at_source)
        def _():
            pltpu.make_async_copy(own_at(i), cross_at(y, i), here_recv.at[i]).wait()

        @pl.when(has_up & (z >= feat))
        def _():
            send(own_at(i), cross_at(y, i), up_send.at[i], here_recv.at[i], to_up).wait_send()

        @pl.when(has_down & (z <= feat))
        def _():
            send(own_at(i), cross_at(y, i), down_send.at[i], here_recv.at[i], to_down).wait_send()

        side = send(own_at(i), cross_at(1 - y, i), side_send.at[i], there_recv.at[i], to_y)
        side.wait_send()
        side.wait_recv()


def gather(kernel, train, test):
    blk, tst, trn = kernel.shape[0], test.shape[0], train.shape[0]
    n_shared = (blk + tst) // CHUNK
    n_own = (blk + tst + trn) // CHUNK
    n_w = SPAN // PIECE
    dma = pltpu.SemaphoreType.DMA
    anywhere = pl.BlockSpec(memory_space=pl.ANY)
    return pl.pallas_call(
        gather_kernel,
        out_shape=(
            jax.ShapeDtypeStruct((blk + tst + trn, SPAN), jnp.float32),
            jax.ShapeDtypeStruct((2, blk + tst, SPAN), jnp.float32),
            jax.ShapeDtypeStruct((SPAN, SPAN), jnp.float32),
        ),
        in_specs=[anywhere] * 3,
        out_specs=(anywhere,) * 3,
        scratch_shapes=[
            pltpu.VMEM((SPAN, SPAN), jnp.float32),
            pltpu.VMEM((SPAN, SPAN), jnp.float32),
            dma((n_own,)), dma((n_own,)), dma((n_own,)),
            dma((n_shared,)), dma((n_shared,)), dma((n_shared,)), dma((n_shared,)), dma((n_shared,)),
            dma((n_w,)), dma((n_w,)), dma((n_w,)), dma((n_w,)), dma((n_w,)), dma((n_w,)),
            dma((n_own,)), dma,
        ],
        compiler_params=pltpu.CompilerParams(
            collective_id=0, has_side_effects=True, vmem_limit_bytes=44 * 1024 * 1024
        ),
    )(kernel, train, test)


def fast(left, right):
    return lax.dot_general(
        left, right, (((1,), (1,)), ((), ())), precision=lax.Precision.HIGH, preferred_element_type=jnp.float32
    )


def per_device(kernel, train_feats, test_feats):
    blk, blk_cols = kernel.shape
    tst, trn = test_feats.shape[0], train_feats.shape[0]
    row_ids = lax.axis_index("rows") * blk + lax.broadcasted_iota(jnp.int32, (blk, 1), 0)
    col_ids = lax.axis_index("feat") * blk_cols + lax.broadcasted_iota(jnp.int32, (1, blk_cols), 1)
    own, cross, winv = gather(kernel, train_feats, test_feats)
    coords = fast(own, winv)
    panel_of = (jnp.arange(SPAN, dtype=jnp.int32) // PANEL) * PANEL
    left = jnp.where(row_ids >= panel_of[None, :], coords[:blk], 0.0)
    test_coords, train_coords = coords[blk : blk + tst], coords[blk + tst :]
    other = fast(cross.reshape(2 * (blk + tst), SPAN), winv).reshape(2, blk + tst, SPAN)
    right = other[:, :blk].reshape(2 * blk, SPAN)
    scored = other[:, blk:].reshape(2 * tst, SPAN)

    def updated(state, part):
        rest = state - fast(part, right)
        padded = jnp.pad(part, ((0, 0), (0, blk_cols - SPAN)))
        return jnp.where(col_ids < SPAN, padded, rest)

    matrix = jnp.where((row_ids < SPAN) & (col_ids >= SPAN), 0.0, updated(kernel, left))
    return (
        matrix,
        updated(train_feats, train_coords),
        updated(test_feats, test_coords),
        fast(train_coords, scored),
    )


def solution(mesh):
    wide = mesh.shape["feat"] == 4 and mesh.shape["rows"] == 8
    return jax.shard_map(
        per_device if wide else general,
        mesh=mesh,
        in_specs=(P("rows", "feat"), P("rows", "feat"), P("rows", "feat")),
        out_specs=(P("rows", "feat"), P("rows", "feat"), P("rows", "feat"), P("rows", "feat")),
        check_vma=False,
    )
```
